512 devices in a mesh: cuts: 8 (over z_lo), fsdp: 64 (over x, z_hi, y, core).
Axes of the slice: x: 4, y: 4, z: 16 (z_hi: 2, z_lo: 8; z = z_hi * 8 + z_lo), core: 2. Of those that a mesh axis runs over, the one named last changes fastest.
Arguments:
- activations: bfloat16 [81920, 1536], P(('cuts', 'fsdp')), may hold values from -6 to 6
- cotangent: bfloat16 [81920, 2048], P(('cuts', 'fsdp')), may hold values from -0.01953125 to 0.01953125
- weights: bfloat16 [1536, 2048], P('fsdp'), may hold values from -0.15625 to 0.15625
- first_moment: float32 [1536, 2048], P('fsdp'), may hold values from -4 to 4
- second_moment: float32 [1536, 2048], P('fsdp'), may hold values from 0.05 to 2
- residue: float32 [8, 1536, 2048], P('cuts', 'fsdp'), may hold values from -3 to 3
Outputs:
- projected: bfloat16 [81920, 2048], P(('cuts', 'fsdp'))
- new_first: float32 [1536, 2048], P('fsdp')
- new_second: float32 [1536, 2048], P('fsdp')
The draws below stay inside these ranges and needn't reach their ends.
All inputs are finite; a program needn't handle non-finite values.
Results may differ from the reference program's by a relative error of at most 0.0049.
Values may be sent and summed in bfloat16 or wider, within the bound.
No kernel may reach another device: no remote copies, remote signals or barrier semaphores. Data moves between devices by JAX's collectives and lax.ppermute only.
A program may use at most 64 MiB of HBM per device.

```python
import math
import jax
import jax.numpy as jnp
from jax import lax

D_W = 1536
HEADS = 8
HEAD_SIZE = 256
TOK_DEV = 160
C = 2048
TOKENS = 81920
N_CUTS = 8
N_FSDP = 64


def level_of(key, extent, split, low, largest):
    factor_of = 1.0
    for position, blocks in split:
        heights = jax.random.uniform(jax.random.fold_in(jax.random.fold_in(key, 6), position), (blocks,), jnp.float32, low / len(split), largest / len(split))
        factor_of = factor_of * jnp.repeat(jnp.exp(heights), extent[position] // blocks).reshape((-1,) + (1,) * (len(extent) - 1 - position))
    return factor_of


def scatter_about(own_key, extent, spread, bound, pieces=(), dtype=jnp.bfloat16):
    result = jax.random.normal(own_key, extent, jnp.float32) * spread
    if len(pieces) > 0:
        result = level_of(own_key, extent, pieces, -0.22, 0.18) * result
    return jnp.clip(result, min=-bound, max=bound).astype(dtype)


def setup_inputs(seed: int = 0) -> dict:
    key_list = jax.random.split(jax.random.key(seed), 7)
    return {
        "activations": scatter_about(key_list[0], (TOKENS, D_W), 1.0, 6.0, ((0, 512),)),
        "cotangent": scatter_about(key_list[1], (TOKENS, C), (TOK_DEV * N_FSDP * N_CUTS) ** -0.5, 0.01953125, ((0, 512),)),
        "weights": scatter_about(key_list[2], (D_W, C), D_W ** -0.5, 0.15625, ((0, 64),)),
        "first_moment": scatter_about(key_list[3], (D_W, C), 0.5, 4.0, ((0, 64),), jnp.float32),
        "second_moment": jnp.clip(jnp.exp(math.log(2.0) - 3.6888794 * jax.random.uniform(key_list[4], (D_W, C), jnp.float32) ** level_of(key_list[4], (D_W, C), ((0, 64),), -0.2, 0.2)), 0.05, 2.0),
        "residue": scatter_about(key_list[5], (N_CUTS, D_W, C), 0.3, 3.0, ((0, 8), (1, 64)), jnp.float32),
    }


def reference(activations, cotangent, weights, first_moment, second_moment, residue):
    acts_all = activations.reshape(N_CUTS, N_FSDP, TOK_DEV, D_W)
    cots_all = cotangent.reshape(N_CUTS, N_FSDP, TOK_DEV, C)

    def slice_total(pair):

        def add_term(total, item):
            term = lax.dot_general(item[0], item[1], (((0,), (0,)), ((), ())), preferred_element_type=jnp.float32)
            rounded = lax.optimization_barrier(term.astype(jnp.bfloat16))
            return (total + rounded.astype(jnp.float32), None)
        total, unused = lax.scan(add_term, jnp.zeros((D_W, C), jnp.float32), (pair[0], pair[1]))
        return total
    slice_grad = lax.map(slice_total, (acts_all, cots_all))
    combined = slice_grad + residue
    blocks = combined.reshape(N_CUTS, D_W, HEADS, HEAD_SIZE)
    scale_low = (lax.optimization_barrier(jnp.max(jnp.abs(blocks), axis=-1)) + 1e-06).astype(jnp.bfloat16)
    scale = lax.optimization_barrier(scale_low).astype(jnp.float32)
    codes = (blocks / scale[..., None]).astype(jnp.bfloat16)
    grad = lax.optimization_barrier(jnp.sum(codes.astype(jnp.float32) * scale[..., None], axis=0)).reshape(D_W, C)
    new_first = 0.9 * first_moment + 0.1 * grad
    new_second = 0.95 * second_moment + 0.05 * grad * grad
    update = new_first / (1.0 - 0.9 ** 10) / (jnp.sqrt(new_second / (1.0 - 0.95 ** 10)) + 1e-08)
    new_weights = (weights.astype(jnp.float32) * (1.0 - 0.002 * 0.1) - 0.002 * update).astype(jnp.bfloat16)
    projected = jnp.dot(activations, new_weights, preferred_element_type=jnp.float32).astype(jnp.bfloat16)
    return (projected, new_first, new_second)
```

```python
import jax
import jax.numpy as jnp
from jax import lax
from jax.sharding import Mesh, PartitionSpec as P

HEAD_SIZE = 256
BF16 = jnp.bfloat16
F32 = jnp.float32


def update_of(grad, first, second, weight):
    new_first = 0.9 * first + 0.1 * grad
    new_second = 0.95 * second + 0.05 * grad * grad
    update = new_first / (1.0 - 0.9**10) / (jnp.sqrt(new_second / (1.0 - 0.95**10)) + 1e-08)
    new_weight = weight.astype(F32) * (1.0 - 0.002 * 0.1) - 0.002 * update
    return new_first, new_second, new_weight.astype(BF16)


def relay(act, cot, weight, first, second, residue):
    nx, ny, nz, nzh = (lax.axis_size(a) for a in ("x", "y", "zl", "zh"))
    core, zh, zl = (lax.axis_index(a) for a in ("core", "zh", "zl"))
    tok, width = cot.shape
    own = weight.shape[0]
    heads = width // HEAD_SIZE
    per = heads // nz * HEAD_SIZE
    rows = nzh * own
    swap = [(0, 1), (1, 0)]

    turned = act.T.reshape(nx, nzh, ny, 2, own, tok).transpose(3, 0, 2, 1, 4, 5)
    turned = turned.reshape(2, nx * ny * rows, tok)
    mine = lax.dynamic_index_in_dim(turned, core, 0, keepdims=False)
    other = lax.dynamic_index_in_dim(turned, 1 - core, 0, keepdims=False)
    other_act = lax.ppermute(other, "core", swap)
    other_cot = lax.ppermute(cot, "core", swap)

    def columns(a):
        return lax.dynamic_slice_in_dim(a, zl * per, per, 1)

    states = jnp.stack([columns(first), columns(second), columns(weight).astype(F32)])
    far = lax.ppermute(states, "zh", swap)
    both = jnp.stack([jnp.where(zh == 0, states, far), jnp.where(zh == 0, far, states)], axis=1)
    both = both.reshape(3, rows, per)

    term = jnp.dot(mine, cot, preferred_element_type=F32)
    term = term + jnp.dot(other_act, other_cot, preferred_element_type=F32)
    pieces = term.astype(BF16).reshape(nx * ny, rows, width)
    arrived = lax.all_to_all(pieces, ("x", "y"), split_axis=0, concat_axis=0, tiled=True)
    part = jnp.sum(arrived, axis=0, dtype=F32).reshape(nzh, own, width)
    here = (jnp.arange(nzh) == zh)[:, None, None]
    part = part + jnp.where(here, residue, 0.0)

    part = part.astype(BF16).reshape(rows, nz, per).transpose(1, 0, 2)
    part = jnp.broadcast_to(part[:, None], (nz, nzh, rows, per)).reshape(nz * nzh, rows, per)
    parts = lax.all_to_all(part, ("zl", "zh"), split_axis=0, concat_axis=0, tiled=True)
    combined = jnp.sum(parts.reshape(nz, nzh, rows, per), axis=1, dtype=F32)
    blocks = combined.reshape(nz, rows, per // HEAD_SIZE, HEAD_SIZE)
    scale = (jnp.max(jnp.abs(blocks), axis=-1) + 1e-06).astype(BF16).astype(F32)
    codes = (blocks / scale[..., None]).astype(BF16)
    grad = jnp.sum(codes.astype(F32) * scale[..., None], axis=0).reshape(rows, per)
    _, _, new_part = update_of(grad, both[0], both[1], both[2])

    own_grad = lax.dynamic_slice_in_dim(grad, zh * own, own, 0)
    high = lax.reduce_precision(own_grad, 8, 7)
    low = (own_grad - high).astype(BF16)
    packed = jnp.concatenate([new_part, high.astype(BF16), low], axis=0)
    packed = jnp.broadcast_to(packed[None], (nz,) + packed.shape)
    packed = lax.all_to_all(packed, "zl", split_axis=0, concat_axis=0, tiled=True)
    spread = packed.transpose(1, 0, 2).reshape(rows + 2 * own, width)
    full_grad = spread[rows : rows + own].astype(F32) + spread[rows + own :].astype(F32)
    new_first, new_second, _ = update_of(full_grad, first, second, weight)

    sent = jnp.broadcast_to(spread[None, :rows], (nx * ny, rows, width))
    new_weights = lax.all_to_all(sent, ("x", "y"), split_axis=0, concat_axis=0, tiled=True)
    new_weights = new_weights.reshape(nx * ny * rows, width)

    def project(turned_act):
        return lax.dot_general(
            turned_act, new_weights, (((0,), (0,)), ((), ())), preferred_element_type=F32
        )

    other_out = lax.ppermute(project(other_act).astype(BF16), "core", swap)
    projected = project(mine) + other_out.astype(F32)
    return projected.astype(BF16), new_first, new_second


def solution(mesh):
    names = ("zl", "x", "zh", "y", "core")
    fine = Mesh(mesh.devices.reshape(8, 4, 2, 4, 2), names)
    fsdp = ("x", "zh", "y", "core")
    in_specs = (P(names, None), P(names, None), P(fsdp, None), P(fsdp, None), P(fsdp, None), P("zl", fsdp, None))
    out_specs = (P(names, None), P(fsdp, None), P(fsdp, None))
    return jax.shard_map(relay, mesh=fine, in_specs=in_specs, out_specs=out_specs, check_vma=False)
```

```python
import jax
import jax.numpy as jnp
from jax import lax
from jax.sharding import Mesh, PartitionSpec as P

HEAD_SIZE = 256
BF16 = jnp.bfloat16
F32 = jnp.float32


def update_of(grad, first, second, weight):
    new_first = 0.9 * first + 0.1 * grad
    new_second = 0.95 * second + 0.05 * grad * grad
    update = new_first / (1.0 - 0.9**10) / (jnp.sqrt(new_second / (1.0 - 0.95**10)) + 1e-08)
    new_weight = weight.astype(F32) * (1.0 - 0.002 * 0.1) - 0.002 * update
    return new_first, new_second, new_weight.astype(BF16)


def exchange(pieces, axes):
    return lax.all_to_all(pieces, axes, split_axis=0, concat_axis=0, tiled=True)


def relay(act, cot, weight, first, second, residue):
    nx, ny, nz, nzh = (lax.axis_size(a) for a in ("x", "y", "zl", "zh"))
    core, zh, zl = (lax.axis_index(a) for a in ("core", "zh", "zl"))
    tok, width = cot.shape
    depth = act.shape[1]
    own = weight.shape[0]
    per = width // nz
    rows = nzh * own
    swap = [(0, 1), (1, 0)]

    all_act = lax.all_gather(act, ("y", "core"), axis=0, tiled=True)

    turned = act.T.reshape(nx, nzh, ny, 2, own, tok).transpose(3, 0, 2, 1, 4, 5)
    turned = turned.reshape(2, nx * ny * rows, tok)
    mine = lax.dynamic_index_in_dim(turned, core, 0, keepdims=False)
    other = lax.dynamic_index_in_dim(turned, 1 - core, 0, keepdims=False)
    other_act = lax.ppermute(other, "core", swap)
    other_cot = lax.ppermute(cot, "core", swap)

    def columns(a):
        return lax.dynamic_slice_in_dim(a, zl * per, per, 1)

    states = jnp.stack([columns(first), columns(second), columns(weight).astype(F32)])
    far = lax.ppermute(states, "zh", swap)

    term = jnp.dot(mine, cot, preferred_element_type=F32)
    term = term + jnp.dot(other_act, other_cot, preferred_element_type=F32)
    pieces = term.astype(BF16).reshape(nx, ny * rows, width)
    arrived = exchange(pieces, "x")
    arrived, far = lax.optimization_barrier((arrived, far))
    part = jnp.sum(arrived, axis=0, dtype=F32).astype(BF16).reshape(ny, rows, width)
    arrived = exchange(part, "y")
    part = jnp.sum(arrived, axis=0, dtype=F32).reshape(nzh, own, width)
    here = (jnp.arange(nzh) == zh)[:, None, None]
    part = part + jnp.where(here, residue, 0.0)

    part = part.astype(BF16).reshape(rows, nz, per).transpose(1, 0, 2)
    part = jnp.broadcast_to(part[:, None], (nz, nzh, rows, per)).reshape(nz * nzh, rows, per)
    parts = exchange(part, ("zl", "zh"))
    combined = jnp.sum(parts.reshape(nz, nzh, rows, per), axis=1, dtype=F32)
    blocks = combined.reshape(nz, rows, per // HEAD_SIZE, HEAD_SIZE)
    scale = (jnp.max(jnp.abs(blocks), axis=-1) + 1e-06).astype(BF16).astype(F32)
    codes = (blocks / scale[..., None]).astype(BF16)
    grad = jnp.sum(codes.astype(F32) * scale[..., None], axis=0).reshape(rows, per)
    both = jnp.stack([jnp.where(zh == 0, states, far), jnp.where(zh == 0, far, states)], axis=1)
    both = both.reshape(3, rows, per)
    _, _, new_part = update_of(grad, both[0], both[1], both[2])

    own_grad = lax.dynamic_slice_in_dim(grad, zh * own, own, 0)
    high = lax.reduce_precision(own_grad, 8, 7)
    low = (own_grad - high).astype(BF16)
    packed = jnp.concatenate([new_part, high.astype(BF16), low], axis=0)
    packed = exchange(jnp.broadcast_to(packed[None], (nz,) + packed.shape), "zl")
    full_grad = packed[:, rows : rows + own].astype(F32) + packed[:, rows + own :].astype(F32)
    full_grad = full_grad.transpose(1, 0, 2).reshape(own, width)
    new_first, new_second, _ = update_of(full_grad, first, second, weight)

    sent = jnp.broadcast_to(packed[None, :, :rows], (nx, nz, rows, per))
    got = exchange(sent.reshape(nx * nz, rows, per), ("x", "y", "core"))
    head = got.reshape(nx, nz, nzh, own, per).transpose(0, 2, 1, 3, 4).reshape(depth, per)
    out = jnp.dot(all_act, head, preferred_element_type=F32).astype(BF16)
    back = exchange(out.reshape(nz, tok, per), ("y", "core"))
    projected = back.transpose(1, 0, 2).reshape(tok, width)
    return projected, new_first, new_second


def solution(mesh):
    names = ("zl", "x", "zh", "y", "core")
    fine = Mesh(mesh.devices.reshape(8, 4, 2, 4, 2), names)
    fsdp = ("x", "zh", "y", "core")
    by_token, by_row = P(names, None), P(fsdp, None)
    in_specs = (by_token, by_token, by_row, by_row, by_row, P("zl", fsdp, None))
    out_specs = (by_token, by_row, by_row)
    return jax.shard_map(relay, mesh=fine, in_specs=in_specs, out_specs=out_specs, check_vma=False)
```

```python
import jax
import jax.numpy as jnp
from jax import lax
from jax.sharding import Mesh, PartitionSpec as P

HEAD_SIZE = 256
BF16 = jnp.bfloat16
F32 = jnp.float32


def update_of(grad, first, second, weight):
    new_first = 0.9 * first + 0.1 * grad
    new_second = 0.95 * second + 0.05 * grad * grad
    update = new_first / (1.0 - 0.9**10) / (jnp.sqrt(new_second / (1.0 - 0.95**10)) + 1e-08)
    new_weight = weight.astype(F32) * (1.0 - 0.002 * 0.1) - 0.002 * update
    return new_first, new_second, new_weight.astype(BF16)


def exchange(pieces, axes):
    return lax.all_to_all(pieces, axes, split_axis=0, concat_axis=0, tiled=True)


def relay(act, cot, weight, first, second, residue):
    nx, ny, nz, nzh = (lax.axis_size(a) for a in ("x", "y", "zl", "zh"))
    core, y, zh, zl = (lax.axis_index(a) for a in ("core", "y", "zh", "zl"))
    tok, width = cot.shape
    depth = act.shape[1]
    own = weight.shape[0]
    per = width // nz
    rows = nzh * own
    swap = [(0, 1), (1, 0)]

    turned = act.T.reshape(nx, nzh, ny, 2, own, tok).transpose(3, 0, 2, 1, 4, 5)
    turned = turned.reshape(2, nx * ny * rows, tok)
    mine = lax.dynamic_index_in_dim(turned, core, 0, keepdims=False)
    other = lax.dynamic_index_in_dim(turned, 1 - core, 0, keepdims=False)
    other_act = lax.ppermute(other, "core", swap)
    other_cot = lax.ppermute(cot, "core", swap)

    term = jnp.dot(mine, cot, preferred_element_type=F32)
    term = term + jnp.dot(other_act, other_cot, preferred_element_type=F32)
    pieces = term.astype(BF16).reshape(nx, ny * rows, width)

    pieces, act = lax.optimization_barrier((pieces, act))
    arrived = exchange(pieces, "x")
    steps = range(1, ny)
    others = [lax.ppermute(act, "y", [(i, (i + k) % ny) for i in range(ny)]) for k in steps]
    arrived, *others = lax.optimization_barrier((arrived, *others))
    part = jnp.sum(arrived, axis=0, dtype=F32).astype(BF16).reshape(ny, rows, width)

    arrived = exchange(part, "y")
    part = jnp.sum(arrived, axis=0, dtype=F32).reshape(nzh, own, width)
    here = (jnp.arange(nzh) == zh)[:, None, None]
    part = part + jnp.where(here, residue, 0.0)

    part = part.astype(BF16).reshape(nzh, own, nz, per).transpose(2, 0, 1, 3)
    part, act, *others = lax.optimization_barrier((part, act, *others))
    parts = exchange(part.reshape(nz * nzh, own, per), ("zl", "zh"))

    row_act = jnp.zeros((ny, 1, tok, depth), BF16)
    for k, a in enumerate([act, *others]):
        row_act = lax.dynamic_update_slice(row_act, a[None, None], ((y + ny - k) % ny, 0, 0, 0))
    other_row = lax.ppermute(row_act, "core", swap)

    combined = jnp.sum(parts.reshape(nz, nzh, own, per), axis=1, dtype=F32)
    blocks = combined.reshape(nz, own, per // HEAD_SIZE, HEAD_SIZE)
    scale = (jnp.max(jnp.abs(blocks), axis=-1) + 1e-06).astype(BF16).astype(F32)
    codes = (blocks / scale[..., None]).astype(BF16)
    grad = jnp.sum(codes.astype(F32) * scale[..., None], axis=0).reshape(own, per)

    def columns(a):
        return lax.dynamic_slice_in_dim(a, zl * per, per, 1)

    _, _, new_part = update_of(grad, columns(first), columns(second), columns(weight))

    packed = jnp.concatenate([new_part, grad.astype(BF16)], axis=0)
    packed = exchange(jnp.broadcast_to(packed[None], (nz * nzh, 2 * own, per)), ("zl", "zh"))
    packed = packed.reshape(nz, nzh, 2, own, per)
    full_grad = lax.dynamic_index_in_dim(packed[:, :, 1], zh, 1, keepdims=False)
    full_grad = full_grad.astype(F32).transpose(1, 0, 2).reshape(own, width)
    new_first, new_second, _ = update_of(full_grad, first, second, weight)

    sent = packed[:, :, 0].reshape(nz, rows, per)
    sent = jnp.broadcast_to(sent[None], (nx, nz, rows, per)).reshape(nx * nz, rows, per)
    sent, row_act, other_row = lax.optimization_barrier((sent, row_act, other_row))
    got = exchange(sent, ("x", "y", "core"))
    all_act = jnp.zeros((ny, 2, tok, depth), BF16)
    all_act = lax.dynamic_update_slice(all_act, row_act, (0, core, 0, 0))
    all_act = lax.dynamic_update_slice(all_act, other_row, (0, 1 - core, 0, 0))
    all_act = all_act.reshape(ny * 2 * tok, depth)
    head = got.reshape(nx, nz, nzh, own, per).transpose(0, 2, 1, 3, 4).reshape(depth, per)
    out = jnp.dot(all_act, head, preferred_element_type=F32).astype(BF16)
    back = exchange(out.reshape(nz, tok, per), ("y", "core"))
    projected = back.transpose(1, 0, 2).reshape(tok, width)
    return projected, new_first, new_second


def solution(mesh):
    names = ("zl", "x", "zh", "y", "core")
    fine = Mesh(mesh.devices.reshape(8, 4, 2, 4, 2), names)
    fsdp = ("x", "zh", "y", "core")
    by_token, by_row = P(names, None), P(fsdp, None)
    in_specs = (by_token, by_token, by_row, by_row, by_row, P("zl", fsdp, None))
    out_specs = (by_token, by_row, by_row)
    return jax.shard_map(relay, mesh=fine, in_specs=in_specs, out_specs=out_specs, check_vma=False)
```

```python
import jax
import jax.numpy as jnp
from jax import lax
from jax.sharding import Mesh, PartitionSpec as P

HEAD_SIZE = 256
BF16 = jnp.bfloat16
F32 = jnp.float32


def update_of(grad, first, second, weight):
    new_first = 0.9 * first + 0.1 * grad
    new_second = 0.95 * second + 0.05 * grad * grad
    update = new_first / (1.0 - 0.9**10) / (jnp.sqrt(new_second / (1.0 - 0.95**10)) + 1e-08)
    new_weight = weight.astype(F32) * (1.0 - 0.002 * 0.1) - 0.002 * update
    return new_first, new_second, new_weight.astype(BF16)


def exchange(pieces, axes):
    return lax.all_to_all(pieces, axes, split_axis=0, concat_axis=0, tiled=True)


def shift(a, axis, k):
    n = lax.axis_size(axis)
    return lax.ppermute(a, axis, [(i, (i + k) % n) for i in range(n)])


def by_head(a):
    rows, width = a.shape
    return a.reshape(rows, width // HEAD_SIZE, HEAD_SIZE).transpose(1, 0, 2)


def flat(a):
    heads, rows, size = a.shape
    return a.transpose(1, 0, 2).reshape(rows, heads * size)


def pick(a, i):
    return lax.dynamic_slice_in_dim(a, i, 1, 0)


def relay(act, cot, weight, first, second, residue):
    nx, ny, nz, nzh = (lax.axis_size(a) for a in ("x", "y", "zl", "zh"))
    core, y, zh, zl = (lax.axis_index(a) for a in ("core", "y", "zh", "zl"))
    tok, depth = act.shape
    own = weight.shape[0]
    group = ("y", "core")
    swap = [(0, 1), (1, 0)]

    near = [act] + [shift(act, "y", k) for k in range(1, ny)]
    acts = near + [lax.ppermute(a, "core", swap) for a in near]

    pieces = jnp.concatenate([by_head(cot), by_head(residue[0].astype(BF16))], axis=1)
    got = exchange(pieces, group)

    member = [2 * lax.rem(y + ny - j % ny, ny) + (core if j < ny else 1 - core) for j in range(2 * ny)]
    place = [lax.rem(y + ny - m // 2, ny) + ny * jnp.abs(core - m % 2) for m in range(2 * ny)]

    all_act = jnp.concatenate(acts, axis=0)
    head_cot = jnp.concatenate([pick(got, m)[0, :tok] for m in member], axis=0)
    term = lax.dot_general(all_act, head_cot, (((0,), (0,)), ((), ())), preferred_element_type=F32)
    term = term.astype(BF16).reshape(nx, depth // nx, HEAD_SIZE)

    def columns(a):
        return lax.dynamic_slice_in_dim(a, zl * HEAD_SIZE, HEAD_SIZE, 1)

    states = jnp.stack([columns(first), columns(second), columns(weight).astype(F32)])
    turn = [(a * nz + b, b * nz + a) for a in range(nz) for b in range(nz)]
    states = lax.ppermute(states, ("zl", "y", "core"), turn)

    arrived = exchange(term, "x")
    arrived, states = lax.optimization_barrier((arrived, states))
    part = jnp.sum(arrived, axis=0, dtype=F32).reshape(nzh, nz, own, HEAD_SIZE)
    here = (jnp.arange(nzh) == zh)[:, None, None, None]
    part = part + jnp.where(here, got[:, tok:].astype(F32), 0.0)

    part = part.astype(BF16).transpose(1, 0, 2, 3).reshape(nz * nzh, own, HEAD_SIZE)
    parts = exchange(part, ("zl", "zh"))
    combined = jnp.sum(parts.reshape(nz, nzh, own, HEAD_SIZE), axis=1, dtype=F32)
    scale = (jnp.max(jnp.abs(combined), axis=-1) + 1e-06).astype(BF16).astype(F32)
    codes = (combined / scale[..., None]).astype(BF16)
    grad = jnp.sum(codes.astype(F32) * scale[..., None], axis=0)
    _, _, new_part = update_of(grad, states[0], states[1], states[2])

    packed = jnp.concatenate([new_part, grad.astype(BF16)], axis=0)
    packed = exchange(jnp.broadcast_to(packed[None], (nz * nzh, 2 * own, HEAD_SIZE)), ("zl", "zh"))
    packed = packed.reshape(nz, nzh, 2, own, HEAD_SIZE)
    sent = packed[:, :, 0].transpose(1, 0, 2, 3).reshape(depth // nx, HEAD_SIZE)
    sent = jnp.broadcast_to(sent[None], (nx, depth // nx, HEAD_SIZE))
    head_weight = exchange(sent, "x").reshape(depth, HEAD_SIZE)

    out = jnp.dot(all_act, head_weight, preferred_element_type=F32).astype(BF16)
    out = out.reshape(2 * ny, tok, HEAD_SIZE)
    out = jnp.concatenate([pick(out, p) for p in place], axis=0)
    row_grad = lax.dynamic_index_in_dim(packed[:, :, 1], zh, 1, keepdims=False)
    back = exchange(jnp.concatenate([out, row_grad], axis=1), group)
    new_first, new_second, _ = update_of(flat(back[:, tok:]).astype(F32), first, second, weight)
    return flat(back[:, :tok]), new_first, new_second


def solution(mesh):
    names = ("zl", "x", "zh", "y", "core")
    fine = Mesh(mesh.devices.reshape(8, 4, 2, 4, 2), names)
    fsdp = ("x", "zh", "y", "core")
    by_token, by_row = P(names, None), P(fsdp, None)
    in_specs = (by_token, by_token, by_row, by_row, by_row, P("zl", fsdp, None))
    out_specs = (by_token, by_row, by_row)
    return jax.shard_map(relay, mesh=fine, in_specs=in_specs, out_specs=out_specs, check_vma=False)
```

```python
import jax
import jax.numpy as jnp
from jax import lax
from jax.experimental import pallas as pl
from jax.experimental.pallas import tpu as pltpu
from jax.sharding import Mesh, PartitionSpec as P

HEAD_SIZE = 256
BF16 = jnp.bfloat16
F32 = jnp.float32


def update_of(grad, first, second, weight):
    new_first = 0.9 * first + 0.1 * grad
    new_second = 0.95 * second + 0.05 * grad * grad
    update = new_first / (1.0 - 0.9**10) / (jnp.sqrt(new_second / (1.0 - 0.95**10)) + 1e-08)
    new_weight = weight.astype(F32) * (1.0 - 0.002 * 0.1) - 0.002 * update
    return new_first, new_second, new_weight.astype(BF16)


def exchange(pieces, axes):
    return lax.all_to_all(pieces, axes, split_axis=0, concat_axis=0, tiled=True)


def shift(a, axis, k):
    n = lax.axis_size(axis)
    return lax.ppermute(a, axis, [(i, (i + k) % n) for i in range(n)])


def call(body, shape, *args):
    spaces = [pltpu.SMEM if a.dtype == jnp.int32 else pltpu.VMEM for a in args]
    return pl.pallas_call(
        body,
        out_shape=jax.ShapeDtypeStruct(shape, BF16),
        in_specs=[pl.BlockSpec(memory_space=m) for m in spaces],
        out_specs=pl.BlockSpec(memory_space=pltpu.VMEM),
        compiler_params=pltpu.CompilerParams(vmem_limit_bytes=32 << 20),
    )(*args)


def split_heads(cot, residue, out):
    heads, rows, size = out.shape
    tok, own = cot.shape[0], residue.shape[0]
    zeros = jnp.zeros((rows - tok - own, size), F32)
    for h in range(heads):
        at = pl.ds(h * size, size)
        out[h, :tok, :] = cot[:, at]
        out[h, tok:, :] = jnp.concatenate([residue[:, at], zeros], axis=0).astype(BF16)


def head_term(member, *refs):
    *acts, cot, out = refs
    tok = acts[0].shape[0]
    blocks, rows, _ = out.shape
    head_cot = jnp.concatenate([cot[member[j], :tok, :] for j in range(len(acts))], axis=0)
    for i in range(blocks):
        act = jnp.concatenate([a[:, i * rows : (i + 1) * rows] for a in acts], axis=0)
        term = lax.dot_general(act, head_cot, (((0,), (0,)), ((), ())), preferred_element_type=F32)
        out[i] = term.astype(BF16)


def project(member, *refs):
    *acts, weight, grad, out = refs
    tok = acts[0].shape[0]
    for j, a in enumerate(acts):
        block = jnp.dot(a[...], weight[...], preferred_element_type=F32)
        out[member[j], :tok, :] = block.astype(BF16)
    out[:, tok:, :] = grad[...]


def flat(a):
    heads, rows, size = a.shape
    return a.transpose(1, 0, 2).reshape(rows, heads * size)


def relay(act, cot, weight, first, second, residue):
    nx, ny, nz, nzh = (lax.axis_size(a) for a in ("x", "y", "zl", "zh"))
    core, y, zh, zl = (lax.axis_index(a) for a in ("core", "y", "zh", "zl"))
    tok, depth = act.shape
    own = weight.shape[0]
    group = ("y", "core")
    swap = [(0, 1), (1, 0)]

    near = [act] + [shift(act, "y", k) for k in range(1, ny)]
    acts = near + [lax.ppermute(a, "core", swap) for a in near]

    block = -(-(tok + own) // 16) * 16
    got = exchange(call(split_heads, (nz, block, HEAD_SIZE), cot, residue[0]), group)

    member = [2 * lax.rem(y + ny - j % ny, ny) + (core if j < ny else 1 - core) for j in range(2 * ny)]
    member = jnp.stack(member).astype(jnp.int32)
    term = call(head_term, (nx, depth // nx, HEAD_SIZE), member, *acts, got)

    def columns(a):
        return lax.dynamic_slice_in_dim(a, zl * HEAD_SIZE, HEAD_SIZE, 1)

    states = jnp.stack([columns(first), columns(second), columns(weight).astype(F32)])
    turn = [(a * nz + b, b * nz + a) for a in range(nz) for b in range(nz)]
    states = lax.ppermute(states, ("zl", "y", "core"), turn)

    arrived = exchange(term, "x")
    arrived, states = lax.optimization_barrier((arrived, states))
    part = jnp.sum(arrived, axis=0, dtype=F32).reshape(nzh, nz, own, HEAD_SIZE)
    here = (jnp.arange(nzh) == zh)[:, None, None, None]
    part = part + jnp.where(here, got[:, tok : tok + own].astype(F32), 0.0)

    part = part.astype(BF16).transpose(1, 0, 2, 3).reshape(nz * nzh, own, HEAD_SIZE)
    parts = exchange(part, ("zl", "zh"))
    combined = jnp.sum(parts.reshape(nz, nzh, own, HEAD_SIZE), axis=1, dtype=F32)
    scale = (jnp.max(jnp.abs(combined), axis=-1) + 1e-06).astype(BF16).astype(F32)
    codes = (combined / scale[..., None]).astype(BF16)
    grad = jnp.sum(codes.astype(F32) * scale[..., None], axis=0)
    _, _, new_part = update_of(grad, states[0], states[1], states[2])

    packed = jnp.concatenate([new_part, grad.astype(BF16)], axis=0)
    packed = exchange(jnp.broadcast_to(packed[None], (nz * nzh, 2 * own, HEAD_SIZE)), ("zl", "zh"))
    packed = packed.reshape(nz, nzh, 2, own, HEAD_SIZE)
    sent = packed[:, :, 0].transpose(1, 0, 2, 3).reshape(depth // nx, HEAD_SIZE)
    sent = jnp.broadcast_to(sent[None], (nx, depth // nx, HEAD_SIZE))
    head_weight = exchange(sent, "x").reshape(depth, HEAD_SIZE)

    row_grad = lax.dynamic_index_in_dim(packed[:, :, 1], zh, 1, keepdims=False)
    row_grad = jnp.pad(row_grad, ((0, 0), (0, block - tok - own), (0, 0)))
    out = call(project, (nz, block, HEAD_SIZE), member, *acts, head_weight, row_grad)
    back = exchange(out, group)
    new_first, new_second, _ = update_of(
        flat(back[:, tok : tok + own]).astype(F32), first, second, weight
    )
    return flat(back[:, :tok]), new_first, new_second


def solution(mesh):
    names = ("zl", "x", "zh", "y", "core")
    fine = Mesh(mesh.devices.reshape(8, 4, 2, 4, 2), names)
    fsdp = ("x", "zh", "y", "core")
    by_token, by_row = P(names, None), P(fsdp, None)
    in_specs = (by_token, by_token, by_row, by_row, by_row, P("zl", fsdp, None))
    out_specs = (by_token, by_row, by_row)
    return jax.shard_map(relay, mesh=fine, in_specs=in_specs, out_specs=out_specs, check_vma=False)
```

```python
import functools

import jax
import jax.numpy as jnp
from jax import lax
from jax.experimental import pallas as pl
from jax.experimental.pallas import tpu as pltpu
from jax.sharding import Mesh, PartitionSpec as P

HEAD_SIZE = 256
BF16 = jnp.bfloat16
F32 = jnp.float32


def moments(grad, first, second):
    return 0.9 * first + 0.1 * grad, 0.95 * second + 0.05 * grad * grad


def updated(grad, first, second, weight):
    new_first, new_second = moments(grad, first, second)
    update = new_first / (1.0 - 0.9**10) / (jnp.sqrt(new_second / (1.0 - 0.95**10)) + 1e-08)
    new_weight = weight * (1.0 - 0.002 * 0.1) - 0.002 * update
    return new_weight


def exchange(pieces, axes):
    return lax.all_to_all(pieces, axes, split_axis=0, concat_axis=0, tiled=True)


def shift(a, axis, k):
    n = lax.axis_size(axis)
    return lax.ppermute(a, axis, [(i, (i + k) % n) for i in range(n)])


def call(body, shapes, *args, scratch=(), hbm=False):
    spaces = [pltpu.SMEM if a.dtype == jnp.int32 else pltpu.HBM if hbm else pltpu.VMEM for a in args]
    out = pl.BlockSpec(memory_space=pltpu.HBM if hbm else pltpu.VMEM)
    return pl.pallas_call(
        body,
        out_shape=shapes,
        in_specs=[pl.BlockSpec(memory_space=m) for m in spaces],
        out_specs=jax.tree.map(lambda _: out, shapes),
        scratch_shapes=scratch,
        compiler_params=pltpu.CompilerParams(vmem_limit_bytes=32 << 20),
    )(*args)


def split_heads(cot, residue, out, residue_here, rounded, copy_sem, residue_sem, out_sem):
    heads, rows, size = out.shape
    tok, own = cot.shape[0], residue.shape[0]
    load = pltpu.make_async_copy(residue, residue_here, residue_sem)
    load.start()
    copies = []
    for h in range(heads):
        source, target = cot.at[:, pl.ds(h * size, size)], out.at[h, pl.ds(0, tok)]
        copies.append(pltpu.make_async_copy(source, target, copy_sem.at[h]))
        copies[-1].start()
    load.wait()
    zeros = jnp.zeros((rows - tok - own, size), F32)
    for h in range(heads):
        block = residue_here[:, h * size : (h + 1) * size]
        rounded[h] = jnp.concatenate([block, zeros], axis=0).astype(BF16)
    copies.append(pltpu.make_async_copy(rounded, out.at[:, pl.ds(tok, rows - tok)], out_sem))
    copies[-1].start()
    for copy in copies:
        copy.wait()


def head_term(own, places, *refs):
    *acts, cot, out = refs
    tok = acts[0].shape[0]
    blocks, rows, _ = out.shape
    heads = cot.shape[0]
    head_cot = jnp.concatenate([cot[places[j], :tok, :] for j in range(len(acts))], axis=0)
    residue = [cot[h, tok:, :].astype(F32)[:own] for h in range(heads)]
    residue = jnp.concatenate(residue, axis=0)
    part = heads * own
    for i in range(blocks):
        act = jnp.concatenate([a[:, i * rows : (i + 1) * rows] for a in acts], axis=0)
        term = lax.dot_general(act, head_cot, (((0,), (0,)), ((), ())), preferred_element_type=F32)
        for k in range(rows // part):
            mine = jnp.logical_and(places[len(acts)] == i, places[len(acts) + 1] == k)
            at = slice(k * part, (k + 1) * part)
            out[i, at, :] = (term[at] + jnp.where(mine, 1.0, 0.0) * residue).astype(BF16)


def sum_blocks(arrived, out):
    total = arrived[0].astype(F32)
    for i in range(1, arrived.shape[0]):
        total = total + arrived[i].astype(F32)
    members, rows, _ = out.shape
    part = total.shape[0] // 2
    own = rows // 2
    for m in range(members):
        low, high = m * own, part + m * own
        block = jnp.concatenate([total[low : low + own], total[high : high + own]], axis=0)
        out[m] = block.astype(BF16)


def update_rows(parts, states, out):
    own = states.shape[1]
    grad = None
    for c in range(parts.shape[0]):
        both = parts[c].astype(F32)
        combined = both[:own] + both[own:]
        scale = jnp.max(jnp.abs(combined), axis=-1, keepdims=True) + 1e-06
        scale = scale.astype(BF16).astype(F32)
        decoded = (combined / scale).astype(BF16).astype(F32) * scale
        grad = decoded if grad is None else grad + decoded
    weight = updated(grad, states[0], states[1], states[2])
    block = jnp.concatenate([weight, grad], axis=0).astype(BF16)
    for i in range(out.shape[0]):
        out[i] = block


def project(places, *refs):
    *acts, weight, grad, out = refs
    tok = acts[0].shape[0]
    for j, a in enumerate(acts):
        block = jnp.dot(a[...], weight[...], preferred_element_type=F32)
        out[places[j], :tok, :] = block.astype(BF16)
    out[:, tok:, :] = grad[...]


def finish(back, first, second, projected, new_first, new_second):
    heads, _, size = back.shape
    tok, own = projected.shape[0], first.shape[0]
    for h in range(heads):
        at = slice(h * size, (h + 1) * size)
        projected[:, at] = back[h, :tok, :]
        grad = back[h, tok:, :].astype(F32)[:own]
        new_first[:, at], new_second[:, at] = moments(grad, first[:, at], second[:, at])


def relay(act, cot, weight, first, second, residue):
    nx, ny, nz, nzh = (lax.axis_size(a) for a in ("x", "y", "zl", "zh"))
    core, x, y, zh, zl = (lax.axis_index(a) for a in ("core", "x", "y", "zh", "zl"))
    tok, depth = act.shape
    own = weight.shape[0]
    group = ("y", "core")
    swap = [(0, 1), (1, 0)]

    near = [act] + [shift(act, "y", k) for k in range(1, ny)]
    acts = near + [lax.ppermute(a, "core", swap) for a in near]

    block = -(-(tok + own) // 16) * 16
    dma = pltpu.SemaphoreType.DMA
    pieces = call(
        split_heads,
        jax.ShapeDtypeStruct((nz, block, HEAD_SIZE), BF16),
        cot,
        residue[0],
        scratch=(
            pltpu.VMEM(residue.shape[1:], F32),
            pltpu.VMEM((nz, block - tok, HEAD_SIZE), BF16),
            dma((nz,)),
            dma,
            dma,
        ),
        hbm=True,
    )
    got = exchange(pieces, group)

    def columns(a):
        return lax.dynamic_slice_in_dim(a, zl * HEAD_SIZE, HEAD_SIZE, 1)

    states = jnp.stack([columns(first), columns(second), columns(weight).astype(F32)])
    turn = [(a * nz + b, b * nz + a) for a in range(nz) for b in range(nz)]
    states = lax.ppermute(states, ("zl", "y", "core"), turn)

    steps = [(k, m) for m in (core, 1 - core) for k in range(ny)]
    places = jnp.stack([2 * lax.rem(y + ny - k, ny) + m for k, m in steps] + [x, zh])
    places = places.astype(jnp.int32)
    rows = depth // nx
    term = jax.ShapeDtypeStruct((nx, rows, HEAD_SIZE), BF16)
    term = call(functools.partial(head_term, own), term, places, *acts, got)

    arrived = exchange(term, "x")
    arrived, states = lax.optimization_barrier((arrived, states))
    part = call(sum_blocks, jax.ShapeDtypeStruct((nz, nzh * own, HEAD_SIZE), BF16), arrived)

    parts = exchange(part.reshape(nz * nzh, own, HEAD_SIZE), ("zl", "zh"))
    packed = jax.ShapeDtypeStruct((nz * nzh, 2 * own, HEAD_SIZE), BF16)
    packed = call(update_rows, packed, parts.reshape(nz, nzh * own, HEAD_SIZE), states)

    packed, upper = lax.optimization_barrier((packed, zh > 0))
    packed = exchange(packed, ("zl", "zh")).reshape(nz, nzh, 2, own, HEAD_SIZE)
    row_grad = jnp.where(upper, packed[:, 1, 1], packed[:, 0, 1])
    row_grad = jnp.pad(row_grad, ((0, 0), (0, block - tok - own), (0, 0)))
    sent = packed[:, :, 0].transpose(1, 0, 2, 3).reshape(rows, HEAD_SIZE)
    sent = jnp.broadcast_to(sent[None], (nx, rows, HEAD_SIZE))
    sent, row_grad = lax.optimization_barrier((sent, row_grad))
    head_weight = exchange(sent, "x").reshape(depth, HEAD_SIZE)

    out = jax.ShapeDtypeStruct((nz, block, HEAD_SIZE), BF16)
    out = call(project, out, places, *acts, head_weight, row_grad)
    back = exchange(out, group)
    state = jax.ShapeDtypeStruct(first.shape, F32)
    shapes = (jax.ShapeDtypeStruct(cot.shape, BF16), state, state)
    return tuple(call(finish, shapes, back, first, second))


def solution(mesh):
    names = ("zl", "x", "zh", "y", "core")
    fine = Mesh(mesh.devices.reshape(8, 4, 2, 4, 2), names)
    fsdp = ("x", "zh", "y", "core")
    by_token, by_row = P(names, None), P(fsdp, None)
    in_specs = (by_token, by_token, by_row, by_row, by_row, P("zl", fsdp, None))
    out_specs = (by_token, by_row, by_row)
    return jax.shard_map(relay, mesh=fine, in_specs=in_specs, out_specs=out_specs, check_vma=False)
```

```python
import functools

import jax
import jax.numpy as jnp
from jax import lax
from jax.experimental import pallas as pl
from jax.experimental.pallas import tpu as pltpu
from jax.sharding import Mesh, PartitionSpec as P

HEAD_SIZE = 256
BF16 = jnp.bfloat16
F32 = jnp.float32


def moments(grad, first, second):
    return 0.9 * first + 0.1 * grad, 0.95 * second + 0.05 * grad * grad


def updated(grad, first, second, weight):
    new_first, new_second = moments(grad, first, second)
    update = new_first / (1.0 - 0.9**10) / (jnp.sqrt(new_second / (1.0 - 0.95**10)) + 1e-08)
    new_weight = weight * (1.0 - 0.002 * 0.1) - 0.002 * update
    return new_weight


def exchange(pieces, axes):
    return lax.all_to_all(pieces, axes, split_axis=0, concat_axis=0, tiled=True)


def shift(a, axis, k):
    n = lax.axis_size(axis)
    return lax.ppermute(a, axis, [(i, (i + k) % n) for i in range(n)])


def call(body, shapes, *args, scratch=(), hbm=False):
    spaces = [pltpu.SMEM if a.dtype == jnp.int32 else pltpu.HBM if hbm else pltpu.VMEM for a in args]
    out = pl.BlockSpec(memory_space=pltpu.HBM if hbm else pltpu.VMEM)
    return pl.pallas_call(
        body,
        out_shape=shapes,
        in_specs=[pl.BlockSpec(memory_space=m) for m in spaces],
        out_specs=jax.tree.map(lambda _: out, shapes),
        scratch_shapes=scratch,
        compiler_params=pltpu.CompilerParams(vmem_limit_bytes=32 << 20),
    )(*args)


def split_heads(cot, residue, out, residue_here, rounded, copy_sem, residue_sem, out_sem):
    heads, rows, size = out.shape
    tok, own = cot.shape[0], residue.shape[0]
    load = pltpu.make_async_copy(residue, residue_here, residue_sem)
    load.start()
    copies = []
    for h in range(heads):
        source, target = cot.at[:, pl.ds(h * size, size)], out.at[h, pl.ds(0, tok)]
        copies.append(pltpu.make_async_copy(source, target, copy_sem.at[h]))
        copies[-1].start()
    load.wait()
    zeros = jnp.zeros((rows - tok - own, size), F32)
    for h in range(heads):
        block = residue_here[:, h * size : (h + 1) * size]
        rounded[h] = jnp.concatenate([block, zeros], axis=0).astype(BF16)
    copies.append(pltpu.make_async_copy(rounded, out.at[:, pl.ds(tok, rows - tok)], out_sem))
    copies[-1].start()
    for copy in copies:
        copy.wait()


def head_term(own, places, *refs):
    *acts, cot, out = refs
    tok = acts[0].shape[0]
    blocks, rows, _ = out.shape
    heads = cot.shape[0]
    head_cot = jnp.concatenate([cot[places[j], :tok, :] for j in range(len(acts))], axis=0)
    residue = [cot[h, tok:, :].astype(F32)[:own] for h in range(heads)]
    residue = jnp.concatenate(residue, axis=0)
    part = heads * own
    for i in range(blocks):
        act = jnp.concatenate([a[:, i * rows : (i + 1) * rows] for a in acts], axis=0)
        term = lax.dot_general(act, head_cot, (((0,), (0,)), ((), ())), preferred_element_type=F32)
        for k in range(rows // part):
            mine = jnp.logical_and(places[len(acts)] == i, places[len(acts) + 1] == k)
            at = slice(k * part, (k + 1) * part)
            out[i, at, :] = (term[at] + jnp.where(mine, 1.0, 0.0) * residue).astype(BF16)


def sum_blocks(places, arrived, out, total):
    value = arrived[0].astype(F32)
    for i in range(1, arrived.shape[0]):
        value = value + arrived[i].astype(F32)
    total[...] = value
    blocks, rows, _ = out.shape
    own, part = rows // 2, total.shape[0] // 2
    for a in range(blocks):
        low = pl.multiple_of(lax.rem(places[places.shape[0] - 1] + a, blocks) * own, 8)
        pieces = [total[pl.ds(k * part + low, own), :] for k in range(2)]
        out[a] = jnp.concatenate(pieces, axis=0).astype(BF16)


def spread(places, packed, sent, row_grad):
    blocks, pad, size = row_grad.shape
    own = packed.shape[1] // 2
    part = blocks * own
    source = [2 * lax.rem(blocks + m - places[places.shape[0] - 1], blocks) for m in range(blocks)]
    for k in range(2):
        rows = [packed[z + k].astype(F32)[:own] for z in source]
        rows = jnp.concatenate(rows, axis=0).astype(BF16)
        for i in range(sent.shape[0]):
            sent[i, k * part : (k + 1) * part, :] = rows
    zeros = jnp.zeros((pad - own, size), F32)
    for m, z in enumerate(source):
        grad = packed[z + places[places.shape[0] - 2]].astype(F32)[own:]
        row_grad[m] = jnp.concatenate([grad, zeros], axis=0).astype(BF16)


def update_rows(parts, states, out):
    own = states.shape[1]
    grad = None
    for c in range(parts.shape[0]):
        both = parts[c].astype(F32)
        combined = both[:own] + both[own:]
        scale = jnp.max(jnp.abs(combined), axis=-1, keepdims=True) + 1e-06
        scale = scale.astype(BF16).astype(F32)
        decoded = (combined / scale).astype(BF16).astype(F32) * scale
        grad = decoded if grad is None else grad + decoded
    weight = updated(grad, states[0], states[1], states[2])
    block = jnp.concatenate([weight, grad], axis=0).astype(BF16)
    for i in range(out.shape[0]):
        out[i] = block


def project(places, *refs):
    *acts, weight, grad, out = refs
    tok = acts[0].shape[0]
    for j, a in enumerate(acts):
        block = jnp.dot(a[...], weight[...], preferred_element_type=F32)
        out[places[j], :tok, :] = block.astype(BF16)
    out[:, tok:, :] = grad[...]


def finish(back, first, second, projected, new_first, new_second):
    heads, _, size = back.shape
    tok, own = projected.shape[0], first.shape[0]
    for h in range(heads):
        at = slice(h * size, (h + 1) * size)
        projected[:, at] = back[h, :tok, :]
        grad = back[h, tok:, :].astype(F32)[:own]
        new_first[:, at], new_second[:, at] = moments(grad, first[:, at], second[:, at])


def relay(act, cot, weight, first, second, residue):
    nx, ny, nz, nzh = (lax.axis_size(a) for a in ("x", "y", "zl", "zh"))
    core, x, y, zh, zl = (lax.axis_index(a) for a in ("core", "x", "y", "zh", "zl"))
    tok, depth = act.shape
    own = weight.shape[0]
    group = ("y", "core")
    swap = [(0, 1), (1, 0)]

    near = [act] + [shift(act, "y", k) for k in range(1, ny)]
    acts = near + [lax.ppermute(a, "core", swap) for a in near]

    block = -(-(tok + own) // 16) * 16
    dma = pltpu.SemaphoreType.DMA
    pieces = call(
        split_heads,
        jax.ShapeDtypeStruct((nz, block, HEAD_SIZE), BF16),
        cot,
        residue[0],
        scratch=(
            pltpu.VMEM(residue.shape[1:], F32),
            pltpu.VMEM((nz, block - tok, HEAD_SIZE), BF16),
            dma((nz,)),
            dma,
            dma,
        ),
        hbm=True,
    )
    got = exchange(pieces, group)

    me = 2 * y + core
    head = lax.rem(me + nz - zl, nz)

    def columns(a):
        return lax.dynamic_slice_in_dim(a, head * HEAD_SIZE, HEAD_SIZE, 1)

    states = jnp.stack([columns(first), columns(second), columns(weight).astype(F32)])
    turn = [(a * nz + (a + b) % nz, a * nz + b) for a in range(nz) for b in range(nz)]
    states = lax.ppermute(states, ("zl", "y", "core"), turn)

    steps = [(k, m) for m in (core, 1 - core) for k in range(ny)]
    places = jnp.stack([2 * lax.rem(y + ny - k, ny) + m for k, m in steps] + [x, zh, me])
    places = places.astype(jnp.int32)
    rows = depth // nx
    term = jax.ShapeDtypeStruct((nx, rows, HEAD_SIZE), BF16)
    term = call(functools.partial(head_term, own), term, places, *acts, got)

    arrived = exchange(term, "x")
    arrived, states = lax.optimization_barrier((arrived, states))
    part = jax.ShapeDtypeStruct((nz, nzh * own, HEAD_SIZE), BF16)
    total = pltpu.VMEM((rows, HEAD_SIZE), F32)
    part = call(sum_blocks, part, places, arrived, scratch=(total,))

    parts = exchange(part.reshape(nz * nzh, own, HEAD_SIZE), ("zl", "zh"))
    packed = jax.ShapeDtypeStruct((nz * nzh, 2 * own, HEAD_SIZE), BF16)
    packed = call(update_rows, packed, parts.reshape(nz, nzh * own, HEAD_SIZE), states)

    packed = exchange(packed, ("zl", "zh"))
    sent = jax.ShapeDtypeStruct((nx, rows, HEAD_SIZE), BF16)
    row_grad = jax.ShapeDtypeStruct((nz, block - tok, HEAD_SIZE), BF16)
    sent, row_grad = call(spread, (sent, row_grad), places, packed)
    sent, row_grad = lax.optimization_barrier((sent, row_grad))
    head_weight = exchange(sent, "x").reshape(depth, HEAD_SIZE)

    out = jax.ShapeDtypeStruct((nz, block, HEAD_SIZE), BF16)
    out = call(project, out, places, *acts, head_weight, row_grad)
    back = exchange(out, group)
    state = jax.ShapeDtypeStruct(first.shape, F32)
    shapes = (jax.ShapeDtypeStruct(cot.shape, BF16), state, state)
    return tuple(call(finish, shapes, back, first, second))


def solution(mesh):
    names = ("zl", "x", "zh", "y", "core")
    fine = Mesh(mesh.devices.reshape(8, 4, 2, 4, 2), names)
    fsdp = ("x", "zh", "y", "core")
    by_token, by_row = P(names, None), P(fsdp, None)
    in_specs = (by_token, by_token, by_row, by_row, by_row, P("zl", fsdp, None))
    out_specs = (by_token, by_row, by_row)
    return jax.shard_map(relay, mesh=fine, in_specs=in_specs, out_specs=out_specs, check_vma=False)
```

```python
import functools

import jax
import jax.numpy as jnp
from jax import lax
from jax.experimental import pallas as pl
from jax.experimental.pallas import tpu as pltpu
from jax.sharding import Mesh, PartitionSpec as P

HEAD_SIZE = 256
BF16 = jnp.bfloat16
F32 = jnp.float32


def moments(grad, first, second):
    return 0.9 * first + 0.1 * grad, 0.95 * second + 0.05 * grad * grad


def updated(grad, first, second, weight):
    new_first, new_second = moments(grad, first, second)
    update = new_first / (1.0 - 0.9**10) / (jnp.sqrt(new_second / (1.0 - 0.95**10)) + 1e-08)
    new_weight = weight * (1.0 - 0.002 * 0.1) - 0.002 * update
    return new_weight


def exchange(pieces, axes):
    return lax.all_to_all(pieces, axes, split_axis=0, concat_axis=0, tiled=True)


def shift(a, axis, k):
    n = lax.axis_size(axis)
    return lax.ppermute(a, axis, [(i, (i + k) % n) for i in range(n)])


def call(body, shapes, *args, scratch=(), hbm=False):
    spaces = [pltpu.SMEM if a.dtype == jnp.int32 else pltpu.HBM if hbm else pltpu.VMEM for a in args]
    out = pl.BlockSpec(memory_space=pltpu.HBM if hbm else pltpu.VMEM)
    return pl.pallas_call(
        body,
        out_shape=shapes,
        in_specs=[pl.BlockSpec(memory_space=m) for m in spaces],
        out_specs=jax.tree.map(lambda _: out, shapes),
        scratch_shapes=scratch,
        compiler_params=pltpu.CompilerParams(vmem_limit_bytes=32 << 20),
    )(*args)


def split_heads(cot, residue, out, residue_here, rounded, copy_sem, residue_sem, out_sem):
    heads, rows, size = out.shape
    tok, own = cot.shape[0], residue.shape[0]
    load = pltpu.make_async_copy(residue, residue_here, residue_sem)
    load.start()
    copies = []
    for h in range(heads):
        source, target = cot.at[:, pl.ds(h * size, size)], out.at[h, pl.ds(0, tok)]
        copies.append(pltpu.make_async_copy(source, target, copy_sem.at[h]))
        copies[-1].start()
    load.wait()
    zeros = jnp.zeros((rows - tok - own, size), F32)
    for h in range(heads):
        block = residue_here[:, h * size : (h + 1) * size]
        rounded[h] = jnp.concatenate([block, zeros], axis=0).astype(BF16)
    copies.append(pltpu.make_async_copy(rounded, out.at[:, pl.ds(tok, rows - tok)], out_sem))
    copies[-1].start()
    for copy in copies:
        copy.wait()


def head_term(own, places, *refs):
    *acts, cot, out = refs
    tok = acts[0].shape[0]
    blocks, rows, _ = out.shape
    heads = cot.shape[0]
    head_cot = jnp.concatenate([cot[places[j], :tok, :] for j in range(len(acts))], axis=0)
    residue = [cot[h, tok:, :].astype(F32)[:own] for h in range(heads)]
    residue = jnp.concatenate(residue, axis=0)
    part = heads * own
    for i in range(blocks):
        act = jnp.concatenate([a[:, i * rows : (i + 1) * rows] for a in acts], axis=0)
        term = lax.dot_general(act, head_cot, (((0,), (0,)), ((), ())), preferred_element_type=F32)
        for k in range(rows // part):
            mine = jnp.logical_and(places[len(acts)] == i, places[len(acts) + 1] == k)
            at = slice(k * part, (k + 1) * part)
            out[i, at, :] = (term[at] + jnp.where(mine, 1.0, 0.0) * residue).astype(BF16)


def sum_blocks(places, arrived, out, total):
    value = arrived[0].astype(F32)
    for i in range(1, arrived.shape[0]):
        value = value + arrived[i].astype(F32)
    total[...] = value
    blocks, rows, _ = out.shape
    own, part = rows // 2, total.shape[0] // 2
    for a in range(blocks):
        low = pl.multiple_of(lax.rem(places[places.shape[0] - 1] + a, blocks) * own, 8)
        pieces = [total[pl.ds(k * part + low, own), :] for k in range(2)]
        out[a] = jnp.concatenate(pieces, axis=0).astype(BF16)


def spread(places, packed, sent, row_grad):
    blocks, pad, size = row_grad.shape
    own = packed.shape[1] // 2
    part = blocks * own
    source = [2 * lax.rem(blocks + m - places[places.shape[0] - 1], blocks) for m in range(blocks)]
    for k in range(2):
        rows = [packed[z + k].astype(F32)[:own] for z in source]
        rows = jnp.concatenate(rows, axis=0).astype(BF16)
        for i in range(sent.shape[0]):
            sent[i, k * part : (k + 1) * part, :] = rows
    zeros = jnp.zeros((pad - own, size), F32)
    for m, z in enumerate(source):
        grad = packed[z + places[places.shape[0] - 2]].astype(F32)[own:]
        row_grad[m] = jnp.concatenate([grad, zeros], axis=0).astype(BF16)


def update_rows(parts, states, out):
    own = states.shape[1]
    grad = None
    for c in range(parts.shape[0]):
        both = parts[c].astype(F32)
        combined = both[:own] + both[own:]
        scale = jnp.max(jnp.abs(combined), axis=-1, keepdims=True) + 1e-06
        scale = scale.astype(BF16).astype(F32)
        decoded = (combined / scale).astype(BF16).astype(F32) * scale
        grad = decoded if grad is None else grad + decoded
    weight = updated(grad, states[0], states[1], states[2])
    block = jnp.concatenate([weight, grad], axis=0).astype(BF16)
    for i in range(out.shape[0]):
        out[i] = block


def project(places, *refs):
    *acts, weight, grad, out = refs
    tok = acts[0].shape[0]
    for j, a in enumerate(acts):
        block = jnp.dot(a[...], weight[...], preferred_element_type=F32)
        out[places[j], :tok, :] = block.astype(BF16)
    out[:, tok:, :] = grad[...]


def finish(back, first, second, projected, new_first, new_second):
    heads, _, size = back.shape
    tok, own = projected.shape[0], first.shape[0]
    for h in range(heads):
        at = slice(h * size, (h + 1) * size)
        projected[:, at] = back[h, :tok, :]
        grad = back[h, tok:, :].astype(F32)[:own]
        new_first[:, at], new_second[:, at] = moments(grad, first[:, at], second[:, at])


def relay(act, cot, weight, first, second, residue):
    nx, ny, nz, nzh = (lax.axis_size(a) for a in ("x", "y", "zl", "zh"))
    core, x, y, zh, zl = (lax.axis_index(a) for a in ("core", "x", "y", "zh", "zl"))
    tok, depth = act.shape
    own = weight.shape[0]
    group = ("y", "core")
    swap = [(0, 1), (1, 0)]

    near = [act] + [shift(act, "y", k) for k in range(1, ny)]
    acts = near + [lax.ppermute(a, "core", swap) for a in near]

    block = -(-(tok + own) // 16) * 16
    dma = pltpu.SemaphoreType.DMA
    pieces = call(
        split_heads,
        jax.ShapeDtypeStruct((nz, block, HEAD_SIZE), BF16),
        cot,
        residue[0],
        scratch=(
            pltpu.VMEM(residue.shape[1:], F32),
            pltpu.VMEM((nz, block - tok, HEAD_SIZE), BF16),
            dma((nz,)),
            dma,
            dma,
        ),
        hbm=True,
    )
    got = exchange(pieces, group)

    me = 2 * y + core
    head = lax.rem(me + nz - zl, nz)

    def columns(a):
        return lax.dynamic_slice_in_dim(a, head * HEAD_SIZE, HEAD_SIZE, 1)

    states = jnp.stack([columns(first), columns(second), columns(weight).astype(F32)])
    got, states = lax.optimization_barrier((got, states))
    turn = [(a * nz + (a + b) % nz, a * nz + b) for a in range(nz) for b in range(nz)]

    steps = [(k, m) for m in (core, 1 - core) for k in range(ny)]
    places = jnp.stack([2 * lax.rem(y + ny - k, ny) + m for k, m in steps] + [x, zh, me])
    places = places.astype(jnp.int32)
    rows = depth // nx
    term = jax.ShapeDtypeStruct((nx, rows, HEAD_SIZE), BF16)
    term = call(functools.partial(head_term, own), term, places, *acts, got)

    arrived = exchange(term, "x")
    part = jax.ShapeDtypeStruct((nz, nzh * own, HEAD_SIZE), BF16)
    total = pltpu.VMEM((rows, HEAD_SIZE), F32)
    part = call(sum_blocks, part, places, arrived, scratch=(total,))

    part, states = lax.optimization_barrier((part, states))
    parts = exchange(part.reshape(nz * nzh, own, HEAD_SIZE), ("zl", "zh"))
    states = lax.ppermute(states, ("zl", "y", "core"), turn)
    parts, states = lax.optimization_barrier((parts, states))
    packed = jax.ShapeDtypeStruct((nz * nzh, 2 * own, HEAD_SIZE), BF16)
    packed = call(update_rows, packed, parts.reshape(nz, nzh * own, HEAD_SIZE), states)

    packed = exchange(packed, ("zl", "zh"))
    sent = jax.ShapeDtypeStruct((nx, rows, HEAD_SIZE), BF16)
    row_grad = jax.ShapeDtypeStruct((nz, block - tok, HEAD_SIZE), BF16)
    sent, row_grad = call(spread, (sent, row_grad), places, packed)
    sent, row_grad = lax.optimization_barrier((sent, row_grad))
    head_weight = exchange(sent, "x").reshape(depth, HEAD_SIZE)

    out = jax.ShapeDtypeStruct((nz, block, HEAD_SIZE), BF16)
    out = call(project, out, places, *acts, head_weight, row_grad)
    back = exchange(out, group)
    state = jax.ShapeDtypeStruct(first.shape, F32)
    shapes = (jax.ShapeDtypeStruct(cot.shape, BF16), state, state)
    return tuple(call(finish, shapes, back, first, second))


def solution(mesh):
    names = ("zl", "x", "zh", "y", "core")
    fine = Mesh(mesh.devices.reshape(8, 4, 2, 4, 2), names)
    fsdp = ("x", "zh", "y", "core")
    by_token, by_row = P(names, None), P(fsdp, None)
    in_specs = (by_token, by_token, by_row, by_row, by_row, P("zl", fsdp, None))
    out_specs = (by_token, by_row, by_row)
    return jax.shard_map(relay, mesh=fine, in_specs=in_specs, out_specs=out_specs, check_vma=False)
```

```python
import functools

import jax
import jax.numpy as jnp
from jax import lax
from jax.experimental import pallas as pl
from jax.experimental.pallas import tpu as pltpu
from jax.sharding import Mesh, PartitionSpec as P

HEAD_SIZE = 256
BF16 = jnp.bfloat16
F32 = jnp.float32


def moments(grad, first, second):
    return 0.9 * first + 0.1 * grad, 0.95 * second + 0.05 * grad * grad


def updated(grad, first, second, weight):
    new_first, new_second = moments(grad, first, second)
    update = new_first / (1.0 - 0.9**10) / (jnp.sqrt(new_second / (1.0 - 0.95**10)) + 1e-08)
    new_weight = weight * (1.0 - 0.002 * 0.1) - 0.002 * update
    return new_weight


def exchange(pieces, axes):
    return lax.all_to_all(pieces, axes, split_axis=0, concat_axis=0, tiled=True)


def shift(a, axis, k):
    n = lax.axis_size(axis)
    return lax.ppermute(a, axis, [(i, (i + k) % n) for i in range(n)])


def call(body, shapes, *args, scratch=(), hbm=False):
    spaces = [pltpu.SMEM if a.dtype == jnp.int32 else pltpu.HBM if hbm else pltpu.VMEM for a in args]
    out = pl.BlockSpec(memory_space=pltpu.HBM if hbm else pltpu.VMEM)
    return pl.pallas_call(
        body,
        out_shape=shapes,
        in_specs=[pl.BlockSpec(memory_space=m) for m in spaces],
        out_specs=jax.tree.map(lambda _: out, shapes),
        scratch_shapes=scratch,
        compiler_params=pltpu.CompilerParams(vmem_limit_bytes=32 << 20),
    )(*args)


def split_heads(cot, residue, out, residue_here, rounded, copy_sem, residue_sem, out_sem):
    heads, rows, size = out.shape
    tok, own = cot.shape[0], residue.shape[0]
    load = pltpu.make_async_copy(residue, residue_here, residue_sem)
    load.start()
    copies = []
    for h in range(heads):
        source, target = cot.at[:, pl.ds(h * size, size)], out.at[h, pl.ds(0, tok)]
        copies.append(pltpu.make_async_copy(source, target, copy_sem.at[h]))
        copies[-1].start()
    load.wait()
    zeros = jnp.zeros((rows - tok - own, size), F32)
    for h in range(heads):
        block = residue_here[:, h * size : (h + 1) * size]
        rounded[h] = jnp.concatenate([block, zeros], axis=0).astype(BF16)
    copies.append(pltpu.make_async_copy(rounded, out.at[:, pl.ds(tok, rows - tok)], out_sem))
    copies[-1].start()
    for copy in copies:
        copy.wait()


def head_term(own, places, *refs):
    *acts, cot, out = refs
    tok = acts[0].shape[0]
    blocks, rows, _ = out.shape
    heads = cot.shape[0]
    head_cot = jnp.concatenate([cot[places[j], :tok, :] for j in range(len(acts))], axis=0)
    residue = [cot[h, tok:, :].astype(F32)[:own] for h in range(heads)]
    residue = jnp.concatenate(residue, axis=0)
    part = heads * own
    for i in range(blocks):
        act = jnp.concatenate([a[:, i * rows : (i + 1) * rows] for a in acts], axis=0)
        term = lax.dot_general(act, head_cot, (((0,), (0,)), ((), ())), preferred_element_type=F32)
        for k in range(rows // part):
            mine = jnp.logical_and(places[len(acts)] == i, places[len(acts) + 1] == k)
            at = slice(k * part, (k + 1) * part)
            out[i, at, :] = (term[at] + jnp.where(mine, 1.0, 0.0) * residue).astype(BF16)


def sum_blocks(places, arrived, out, total):
    value = arrived[0].astype(F32)
    for i in range(1, arrived.shape[0]):
        value = value + arrived[i].astype(F32)
    total[...] = value
    blocks, rows, _ = out.shape
    own, part = rows // 2, total.shape[0] // 2
    for a in range(blocks):
        low = pl.multiple_of(lax.rem(places[places.shape[0] - 1] + a, blocks) * own, 8)
        pieces = [total[pl.ds(k * part + low, own), :] for k in range(2)]
        out[a] = jnp.concatenate(pieces, axis=0).astype(BF16)


def spread(places, packed, sent, row_grad):
    blocks, pad, size = row_grad.shape
    own = packed.shape[1] // 2
    part = blocks * own
    source = [2 * lax.rem(blocks + m - places[places.shape[0] - 1], blocks) for m in range(blocks)]
    for k in range(2):
        rows = [packed[z + k].astype(F32)[:own] for z in source]
        rows = jnp.concatenate(rows, axis=0).astype(BF16)
        for i in range(sent.shape[0]):
            sent[i, k * part : (k + 1) * part, :] = rows
    zeros = jnp.zeros((pad - own, size), F32)
    for m, z in enumerate(source):
        grad = packed[z + places[places.shape[0] - 2]].astype(F32)[own:]
        row_grad[m] = jnp.concatenate([grad, zeros], axis=0).astype(BF16)


def update_rows(parts, states, out):
    own = states.shape[1]
    grad = None
    for c in range(parts.shape[0]):
        both = parts[c].astype(F32)
        combined = both[:own] + both[own:]
        scale = jnp.max(jnp.abs(combined), axis=-1, keepdims=True) + 1e-06
        scale = scale.astype(BF16).astype(F32)
        decoded = (combined / scale).astype(BF16).astype(F32) * scale
        grad = decoded if grad is None else grad + decoded
    weight = updated(grad, states[0], states[1], states[2])
    block = jnp.concatenate([weight, grad], axis=0).astype(BF16)
    for i in range(out.shape[0]):
        out[i] = block


def project(places, *refs):
    *acts, weight, grad, out = refs
    tok = acts[0].shape[0]
    for j, a in enumerate(acts):
        block = jnp.dot(a[...], weight[...], preferred_element_type=F32)
        out[places[j], :tok, :] = block.astype(BF16)
    out[:, tok:, :] = grad[...]


def finish(back, first, second, projected, new_first, new_second):
    heads, _, size = back.shape
    tok, own = projected.shape[0], first.shape[0]
    for h in range(heads):
        at = slice(h * size, (h + 1) * size)
        projected[:, at] = back[h, :tok, :]
        grad = back[h, tok:, :].astype(F32)[:own]
        new_first[:, at], new_second[:, at] = moments(grad, first[:, at], second[:, at])


def relay(act, cot, weight, first, second, residue):
    nx, ny, nz, nzh = (lax.axis_size(a) for a in ("x", "y", "zl", "zh"))
    core, x, y, zh, zl = (lax.axis_index(a) for a in ("core", "x", "y", "zh", "zl"))
    tok, depth = act.shape
    own = weight.shape[0]
    group = ("y", "core")
    swap = [(0, 1), (1, 0)]

    block = -(-(tok + own) // 16) * 16
    dma = pltpu.SemaphoreType.DMA
    pieces = call(
        split_heads,
        jax.ShapeDtypeStruct((nz, block, HEAD_SIZE), BF16),
        cot,
        residue[0],
        scratch=(
            pltpu.VMEM(residue.shape[1:], F32),
            pltpu.VMEM((nz, block - tok, HEAD_SIZE), BF16),
            dma((nz,)),
            dma,
            dma,
        ),
        hbm=True,
    )
    pieces, late = lax.optimization_barrier((pieces, act))
    got = exchange(pieces, group)

    near = [act] + [shift(late if k == 2 else act, "y", k) for k in range(1, ny)]
    acts = near + [lax.ppermute(a, "core", swap) for a in near]

    me = 2 * y + core
    head = lax.rem(me + nz - zl, nz)

    def columns(a):
        return lax.dynamic_slice_in_dim(a, head * HEAD_SIZE, HEAD_SIZE, 1)

    states = jnp.stack([columns(first), columns(second), columns(weight).astype(F32)])
    got, states = lax.optimization_barrier((got, states))
    turn = [(a * nz + (a + b) % nz, a * nz + b) for a in range(nz) for b in range(nz)]

    steps = [(k, m) for m in (core, 1 - core) for k in range(ny)]
    places = jnp.stack([2 * lax.rem(y + ny - k, ny) + m for k, m in steps] + [x, zh, me])
    places = places.astype(jnp.int32)
    rows = depth // nx
    term = jax.ShapeDtypeStruct((nx, rows, HEAD_SIZE), BF16)
    term = call(functools.partial(head_term, own), term, places, *acts, got)

    arrived = exchange(term, "x")
    part = jax.ShapeDtypeStruct((nz, nzh * own, HEAD_SIZE), BF16)
    total = pltpu.VMEM((rows, HEAD_SIZE), F32)
    part = call(sum_blocks, part, places, arrived, scratch=(total,))

    part, states = lax.optimization_barrier((part, states))
    parts = exchange(part.reshape(nz * nzh, own, HEAD_SIZE), ("zl", "zh"))
    states = lax.ppermute(states, ("zl", "y", "core"), turn)
    parts, states = lax.optimization_barrier((parts, states))
    packed = jax.ShapeDtypeStruct((nz * nzh, 2 * own, HEAD_SIZE), BF16)
    packed = call(update_rows, packed, parts.reshape(nz, nzh * own, HEAD_SIZE), states)

    packed = exchange(packed, ("zl", "zh"))
    sent = jax.ShapeDtypeStruct((nx, rows, HEAD_SIZE), BF16)
    row_grad = jax.ShapeDtypeStruct((nz, block - tok, HEAD_SIZE), BF16)
    sent, row_grad = call(spread, (sent, row_grad), places, packed)
    sent, row_grad = lax.optimization_barrier((sent, row_grad))
    head_weight = exchange(sent, "x").reshape(depth, HEAD_SIZE)

    out = jax.ShapeDtypeStruct((nz, block, HEAD_SIZE), BF16)
    out = call(project, out, places, *acts, head_weight, row_grad)
    back = exchange(out, group)
    state = jax.ShapeDtypeStruct(first.shape, F32)
    shapes = (jax.ShapeDtypeStruct(cot.shape, BF16), state, state)
    return tuple(call(finish, shapes, back, first, second))


def solution(mesh):
    names = ("zl", "x", "zh", "y", "core")
    fine = Mesh(mesh.devices.reshape(8, 4, 2, 4, 2), names)
    fsdp = ("x", "zh", "y", "core")
    by_token, by_row = P(names, None), P(fsdp, None)
    in_specs = (by_token, by_token, by_row, by_row, by_row, P("zl", fsdp, None))
    out_specs = (by_token, by_row, by_row)
    return jax.shard_map(relay, mesh=fine, in_specs=in_specs, out_specs=out_specs, check_vma=False)
```

```python
import functools

import jax
import jax.numpy as jnp
from jax import lax
from jax.experimental import pallas as pl
from jax.experimental.pallas import tpu as pltpu
from jax.sharding import Mesh, PartitionSpec as P

HEAD_SIZE = 256
BF16 = jnp.bfloat16
F32 = jnp.float32


def moments(grad, first, second):
    return 0.9 * first + 0.1 * grad, 0.95 * second + 0.05 * grad * grad


def updated(grad, first, second, weight):
    new_first, new_second = moments(grad, first, second)
    update = new_first / (1.0 - 0.9**10) / (jnp.sqrt(new_second / (1.0 - 0.95**10)) + 1e-08)
    new_weight = weight * (1.0 - 0.002 * 0.1) - 0.002 * update
    return new_weight


def exchange(pieces, axes):
    return lax.all_to_all(pieces, axes, split_axis=0, concat_axis=0, tiled=True)


def shift(a, axis, k):
    n = lax.axis_size(axis)
    return lax.ppermute(a, axis, [(i, (i + k) % n) for i in range(n)])


def call(body, shapes, *args, scratch=(), hbm=False, stay=()):
    spaces = [pltpu.SMEM if a.dtype == jnp.int32 else pltpu.HBM if hbm else pltpu.VMEM for a in args]
    spaces = [pl.ANY if n in stay else m for n, m in enumerate(spaces)]
    out = pl.BlockSpec(memory_space=pltpu.HBM if hbm else pltpu.VMEM)
    return pl.pallas_call(
        body,
        out_shape=shapes,
        in_specs=[pl.BlockSpec(memory_space=m) for m in spaces],
        out_specs=jax.tree.map(lambda _: out, shapes),
        scratch_shapes=scratch,
        compiler_params=pltpu.CompilerParams(vmem_limit_bytes=32 << 20),
    )(*args)


def split_heads(cot, residue, out, residue_here, rounded, copy_sem, residue_sem, out_sem):
    heads, rows, size = out.shape
    tok, own = cot.shape[0], residue.shape[0]
    load = pltpu.make_async_copy(residue, residue_here, residue_sem)
    load.start()
    copies = []
    for h in range(heads):
        source, target = cot.at[:, pl.ds(h * size, size)], out.at[h, pl.ds(0, tok)]
        copies.append(pltpu.make_async_copy(source, target, copy_sem.at[h]))
        copies[-1].start()
    load.wait()
    zeros = jnp.zeros((rows - tok - own, size), F32)
    for h in range(heads):
        block = residue_here[:, h * size : (h + 1) * size]
        rounded[h] = jnp.concatenate([block, zeros], axis=0).astype(BF16)
    copies.append(pltpu.make_async_copy(rounded, out.at[:, pl.ds(tok, rows - tok)], out_sem))
    copies[-1].start()
    for copy in copies:
        copy.wait()


def head_term(own, places, *refs):
    *acts, cot, out = refs
    tok = acts[0].shape[0]
    blocks, rows, _ = out.shape
    heads = cot.shape[0]
    head_cot = jnp.concatenate([cot[places[j], :tok, :] for j in range(len(acts))], axis=0)
    residue = [cot[h, tok:, :].astype(F32)[:own] for h in range(heads)]
    residue = jnp.concatenate(residue, axis=0)
    part = heads * own
    for i in range(blocks):
        act = jnp.concatenate([a[:, i * rows : (i + 1) * rows] for a in acts], axis=0)
        term = lax.dot_general(act, head_cot, (((0,), (0,)), ((), ())), preferred_element_type=F32)
        for k in range(rows // part):
            mine = jnp.logical_and(places[len(acts)] == i, places[len(acts) + 1] == k)
            at = slice(k * part, (k + 1) * part)
            out[i, at, :] = (term[at] + jnp.where(mine, 1.0, 0.0) * residue).astype(BF16)


def sum_blocks(places, arrived, out, total):
    value = arrived[0].astype(F32)
    for i in range(1, arrived.shape[0]):
        value = value + arrived[i].astype(F32)
    total[...] = value
    blocks, rows, _ = out.shape
    own, part = rows // 2, total.shape[0] // 2
    for a in range(blocks):
        low = pl.multiple_of(lax.rem(places[places.shape[0] - 1] + a, blocks) * own, 8)
        pieces = [total[pl.ds(k * part + low, own), :] for k in range(2)]
        out[a] = jnp.concatenate(pieces, axis=0).astype(BF16)


def spread(places, packed, sent, row_grad):
    blocks, pad, size = row_grad.shape
    own = packed.shape[1] // 2
    part = blocks * own
    source = [2 * lax.rem(blocks + m - places[places.shape[0] - 1], blocks) for m in range(blocks)]
    for k in range(2):
        rows = [packed[z + k].astype(F32)[:own] for z in source]
        rows = jnp.concatenate(rows, axis=0).astype(BF16)
        for i in range(sent.shape[0]):
            sent[i, k * part : (k + 1) * part, :] = rows
    zeros = jnp.zeros((pad - own, size), F32)
    for m, z in enumerate(source):
        grad = packed[z + places[places.shape[0] - 2]].astype(F32)[own:]
        row_grad[m] = jnp.concatenate([grad, zeros], axis=0).astype(BF16)


def update_rows(parts, states, out):
    own = states.shape[1]
    grad = None
    for c in range(parts.shape[0]):
        both = parts[c].astype(F32)
        combined = both[:own] + both[own:]
        scale = jnp.max(jnp.abs(combined), axis=-1, keepdims=True) + 1e-06
        scale = scale.astype(BF16).astype(F32)
        decoded = (combined / scale).astype(BF16).astype(F32) * scale
        grad = decoded if grad is None else grad + decoded
    weight = updated(grad, states[0], states[1], states[2])
    block = jnp.concatenate([weight, grad], axis=0).astype(BF16)
    for i in range(out.shape[0]):
        out[i] = block


def project(places, *refs):
    *acts, weight, grad, out, fetched, sems = refs
    here = len(acts) - fetched.shape[0]
    copies = [
        pltpu.make_async_copy(a, fetched.at[n], sems.at[n]) for n, a in enumerate(acts[here:])
    ]
    for copy in copies:
        copy.start()
    tok = acts[0].shape[0]
    out[:, tok:, :] = grad[...]
    for j in range(len(acts)):
        if j < here:
            act = acts[j][...]
        else:
            copies[j - here].wait()
            act = fetched[j - here]
        block = jnp.dot(act, weight[...], preferred_element_type=F32)
        out[places[j], :tok, :] = block.astype(BF16)


def finish(back, first, second, projected, new_first, new_second):
    heads, _, size = back.shape
    tok, own = projected.shape[0], first.shape[0]
    for h in range(heads):
        at = slice(h * size, (h + 1) * size)
        projected[:, at] = back[h, :tok, :]
        grad = back[h, tok:, :].astype(F32)[:own]
        new_first[:, at], new_second[:, at] = moments(grad, first[:, at], second[:, at])


def relay(act, cot, weight, first, second, residue):
    nx, ny, nz, nzh = (lax.axis_size(a) for a in ("x", "y", "zl", "zh"))
    core, x, y, zh, zl = (lax.axis_index(a) for a in ("core", "x", "y", "zh", "zl"))
    tok, depth = act.shape
    own = weight.shape[0]
    group = ("y", "core")
    swap = [(0, 1), (1, 0)]

    near = [act] + [shift(act, "y", k) for k in range(1, ny)]
    acts = near + [lax.ppermute(a, "core", swap) for a in near]

    block = -(-(tok + own) // 16) * 16
    dma = pltpu.SemaphoreType.DMA
    pieces = call(
        split_heads,
        jax.ShapeDtypeStruct((nz, block, HEAD_SIZE), BF16),
        cot,
        residue[0],
        scratch=(
            pltpu.VMEM(residue.shape[1:], F32),
            pltpu.VMEM((nz, block - tok, HEAD_SIZE), BF16),
            dma((nz,)),
            dma,
            dma,
        ),
        hbm=True,
    )
    got = exchange(pieces, group)

    me = 2 * y + core
    head = lax.rem(me + nz - zl, nz)

    def columns(a):
        return lax.dynamic_slice_in_dim(a, head * HEAD_SIZE, HEAD_SIZE, 1)

    states = jnp.stack([columns(first), columns(second), columns(weight).astype(F32)])
    got, states = lax.optimization_barrier((got, states))
    turn = [(a * nz + (a + b) % nz, a * nz + b) for a in range(nz) for b in range(nz)]

    steps = [(k, m) for m in (core, 1 - core) for k in range(ny)]
    places = jnp.stack([2 * lax.rem(y + ny - k, ny) + m for k, m in steps] + [x, zh, me])
    places = places.astype(jnp.int32)
    rows = depth // nx
    term = jax.ShapeDtypeStruct((nx, rows, HEAD_SIZE), BF16)
    term = call(functools.partial(head_term, own), term, places, *acts, got)

    arrived = exchange(term, "x")
    part = jax.ShapeDtypeStruct((nz, nzh * own, HEAD_SIZE), BF16)
    total = pltpu.VMEM((rows, HEAD_SIZE), F32)
    part = call(sum_blocks, part, places, arrived, scratch=(total,))

    part, states = lax.optimization_barrier((part, states))
    parts = exchange(part.reshape(nz * nzh, own, HEAD_SIZE), ("zl", "zh"))
    states = lax.ppermute(states, ("zl", "y", "core"), turn)
    parts, states = lax.optimization_barrier((parts, states))
    packed = jax.ShapeDtypeStruct((nz * nzh, 2 * own, HEAD_SIZE), BF16)
    packed = call(update_rows, packed, parts.reshape(nz, nzh * own, HEAD_SIZE), states)

    packed = exchange(packed, ("zl", "zh"))
    sent = jax.ShapeDtypeStruct((nx, rows, HEAD_SIZE), BF16)
    row_grad = jax.ShapeDtypeStruct((nz, block - tok, HEAD_SIZE), BF16)
    sent, row_grad = call(spread, (sent, row_grad), places, packed)
    sent, row_grad = lax.optimization_barrier((sent, row_grad))
    head_weight = exchange(sent, "x").reshape(depth, HEAD_SIZE)

    out = jax.ShapeDtypeStruct((nz, block, HEAD_SIZE), BF16)
    fetch = (pltpu.VMEM((ny, tok, depth), BF16), dma((ny,)))
    stay = range(1 + ny, 1 + 2 * ny)
    out = call(project, out, places, *acts, head_weight, row_grad, scratch=fetch, stay=stay)
    back = exchange(out, group)
    state = jax.ShapeDtypeStruct(first.shape, F32)
    shapes = (jax.ShapeDtypeStruct(cot.shape, BF16), state, state)
    return tuple(call(finish, shapes, back, first, second))


def solution(mesh):
    names = ("zl", "x", "zh", "y", "core")
    fine = Mesh(mesh.devices.reshape(8, 4, 2, 4, 2), names)
    fsdp = ("x", "zh", "y", "core")
    by_token, by_row = P(names, None), P(fsdp, None)
    in_specs = (by_token, by_token, by_row, by_row, by_row, P("zl", fsdp, None))
    out_specs = (by_token, by_row, by_row)
    return jax.shard_map(relay, mesh=fine, in_specs=in_specs, out_specs=out_specs, check_vma=False)
```
